256 devices in a mesh: input: 8 (over y_hi, x), freq: 16 (over z, core), tm: 2 (over y_lo).
Axes of the slice: x: 4, y: 4 (y_hi: 2, y_lo: 2; y = y_hi * 2 + y_lo), z: 8, core: 2. Of those that a mesh axis runs over, the one named last changes fastest.
Arguments:
- voltages: bfloat16 [1024, 256, 2048], P(('input', 'freq'), 'tm'), may hold values from -6 to 6
- taps: float32 [4, 2048], replicated, may hold values from -0.09375 to 0.09375
Outputs:
- visibilities: bfloat16 [2, 512, 1024, 1024], P(None, ('input', 'freq'), 'tm')
The draws below stay inside these ranges and needn't reach their ends.
All inputs are finite; a program needn't handle non-finite values.
Results may differ from the reference program's by a relative error of at most 0.012.
Values may be sent and summed in bfloat16 or wider, within the bound.
No kernel may reach another device: no remote copies, remote signals or barrier semaphores. Data moves between devices by JAX's collectives and lax.ppermute only.
A program may use at most 128 MiB of HBM per device.

```python
import math
import jax
import jax.numpy as jnp
from jax import lax

NPT = 2048
CH = 512
TAPS = 4
IN_DEV = 8
NI = 1024
SPECTRA = 256


def shard_levels(own_key, extent, shards, low, largest):
    def one(axis_at, blocks):
        draws = jax.random.uniform(jax.random.fold_in(jax.random.fold_in(own_key, 6), axis_at), (blocks,), jnp.float32, low / len(shards), largest / len(shards))
        return jnp.repeat(jnp.exp(draws), extent[axis_at] // blocks).reshape((-1,) + (1,) * (len(extent) - axis_at - 1))

    factor_of = one(*shards[0])
    for cut in shards[1:]:
        factor_of = factor_of * one(*cut)
    return factor_of


def noise(rng, shape, scale, bound, shards=(), held_as=jnp.bfloat16):
    loudness = shard_levels(rng, shape, shards, -0.22, 0.18) if shards else 1.0
    result = jax.random.normal(rng, shape, jnp.float32) * scale * loudness
    return jnp.minimum(jnp.maximum(result, -bound), bound).astype(held_as)


def setup_inputs(seed: int = 0) -> dict:
    keys = jax.random.split(jax.random.key(seed), 3)
    voltages = noise(keys[0], (NI, SPECTRA, NPT), 1.0, 6.0, ((0, 128), (1, 2)))
    taps = noise(keys[1], (TAPS, NPT), (2 * NPT) ** -0.5, 0.09375, (), jnp.float32)
    return dict(voltages=voltages, taps=taps)


def dft_table():
    chan = jnp.arange(CH, dtype=jnp.int32)[:, None]
    sample = jnp.arange(NPT, dtype=jnp.int32)[None, :]
    phase = (chan * sample) % NPT
    angle = phase.astype(jnp.float32) * (2.0 * math.pi / NPT)
    return jnp.stack([jnp.cos(angle), -jnp.sin(angle)]).astype(jnp.bfloat16)


def reference(voltages, taps):
    table = dft_table().astype(jnp.float32)
    blocks = voltages.reshape(NI // IN_DEV, IN_DEV, SPECTRA, NPT)

    def filter_block(block):
        wide = jnp.pad(block.astype(jnp.float32), ((0, 0), (TAPS - 1, 0), (0, 0)))
        total = jnp.zeros((IN_DEV, SPECTRA, NPT), jnp.float32)
        for lag in range(TAPS):
            total = total + taps[lag] * wide[:, TAPS - 1 - lag:TAPS - 1 - lag + SPECTRA]
        filtered = total.astype(jnp.bfloat16).astype(jnp.float32)
        spectra = jnp.einsum('rcs,its->cirt', table, filtered, precision=lax.Precision.HIGHEST)
        return spectra.astype(jnp.bfloat16)

    spectra = lax.map(filter_block, blocks)
    spectra = jnp.moveaxis(spectra, 0, 1).reshape(CH, NI, 2, SPECTRA)
    scale = 1.0 / SPECTRA

    def correlate(chan):
        real_part = chan[:, 0].astype(jnp.float32)
        imag_part = chan[:, 1].astype(jnp.float32)
        hp = lax.Precision.HIGHEST
        real = jnp.dot(real_part, real_part.T, precision=hp) + jnp.dot(imag_part, imag_part.T, precision=hp)
        imag = jnp.dot(imag_part, real_part.T, precision=hp) - jnp.dot(real_part, imag_part.T, precision=hp)
        return ((real * scale).astype(jnp.bfloat16), (imag * scale).astype(jnp.bfloat16))

    real_all, imag_all = lax.map(correlate, spectra)
    return jnp.stack([real_all, imag_all])
```

```python
import functools
import math

import jax
import jax.numpy as jnp
from jax import lax
from jax.experimental import pallas as pl
from jax.experimental.pallas import tpu as pltpu
from jax.sharding import PartitionSpec as P

CH = 512
LANES = 128
MIB = 1024 * 1024


def passed_along(block, axis, distance):
    devices = range(lax.axis_size(axis))
    route = [(i - distance, i) for i in devices if i - distance in devices]
    return lax.ppermute(block, axis, route)


def swapped(block, axis):
    size = lax.axis_size(axis)
    return lax.ppermute(block, axis, [(i, size - 1 - i) for i in range(size)])


def tables(npoints, groups, per_group):
    half, quarter = npoints // 2, npoints // 4
    unit = 2.0 * math.pi / npoints
    group = lax.broadcasted_iota(jnp.int32, (groups, quarter), 0)
    sample = lax.broadcasted_iota(jnp.int32, (groups, quarter), 1)
    angle = ((per_group * group * sample) % npoints).astype(jnp.float32) * unit
    cos_base, sin_base = jnp.cos(angle), jnp.sin(angle)
    cos_base, sin_base = lax.optimization_barrier((cos_base, sin_base))
    out = [jnp.concatenate([cos_base, -sin_base]).astype(jnp.bfloat16)]
    for j in range(1, per_group):
        depth = quarter if j % 2 == 0 else half
        turn = ((j * jnp.arange(depth, dtype=jnp.int32)) % npoints).astype(jnp.float32) * unit
        cos_turn, sin_turn = jnp.cos(turn), jnp.sin(turn)
        cos_wide = jnp.tile(cos_base, (1, depth // quarter))
        sin_wide = jnp.tile(sin_base, (1, depth // quarter))
        real = cos_wide * cos_turn - sin_wide * sin_turn
        imag = -(sin_wide * cos_turn + cos_wide * sin_turn)
        out.append(jnp.concatenate([real, imag]).astype(jnp.bfloat16))
    return out


def filter_kernel(volt_ref, hist_ref, taps_ref, sum_ref, alt_ref, diff_ref):
    ntaps = taps_ref.shape[0]
    count = volt_ref.shape[1]
    quarter = sum_ref.shape[1]
    nhist = hist_ref.shape[1]
    pad = 8

    def filtered(start):
        lanes = slice(start, start + LANES)
        hist = hist_ref[0, :, lanes].astype(jnp.float32)
        body = volt_ref[0, :, lanes].astype(jnp.float32)
        top = jnp.zeros((pad - nhist, LANES), jnp.float32)
        wide = jnp.concatenate([top, hist, body], axis=0)
        total = taps_ref[ntaps - 1, lanes] * wide
        for lag in range(ntaps - 2, -1, -1):
            total = pltpu.roll(total, 1, 0) + taps_ref[lag, lanes] * wide
        return total[pad:]

    for start in range(0, quarter, LANES):
        here = slice(start, start + LANES)
        first, third = filtered(start), filtered(start + 2 * quarter)
        diff_ref[:, here] = (first - third).astype(jnp.bfloat16)
        even = first + third
        second, fourth = filtered(start + quarter), filtered(start + 3 * quarter)
        there = slice(start + quarter, start + quarter + LANES)
        diff_ref[:, there] = (second - fourth).astype(jnp.bfloat16)
        odd = second + fourth
        sum_ref[:, here] = (even + odd).astype(jnp.bfloat16)
        alt_ref[:, here] = (even - odd).astype(jnp.bfloat16)


def filter_bank(voltages, history, taps):
    width, count, npoints = voltages.shape
    half, quarter = npoints // 2, npoints // 4
    rows = width * count
    depths = (quarter, quarter, half)
    return pl.pallas_call(
        filter_kernel,
        grid=(width,),
        in_specs=[
            pl.BlockSpec((1, count, npoints), lambda i: (i, 0, 0)),
            pl.BlockSpec((1, history.shape[1], npoints), lambda i: (i, 0, 0)),
            pl.BlockSpec(taps.shape, lambda i: (0, 0)),
        ],
        out_specs=[pl.BlockSpec((count, d), lambda i: (i, 0)) for d in depths],
        out_shape=[jax.ShapeDtypeStruct((rows, d), jnp.bfloat16) for d in depths],
        compiler_params=pltpu.CompilerParams(vmem_limit_bytes=48 * MIB),
        cost_estimate=pl.CostEstimate(flops=20 * rows * npoints, bytes_accessed=4 * rows * npoints, transcendentals=0),
        name="filter_bank",
    )(voltages, history, taps)


def spectra_kernel(width, table_ref, filt_ref, out_ref, wide_ref):
    rows = filt_ref.shape[0]
    count = rows // width
    groups = out_ref.shape[0]
    pair = 2 * count
    for step in range(rows // pair):
        product = lax.dot_general(
            table_ref[...], filt_ref[step * pair : (step + 1) * pair, :],
            (((1,), (1,)), ((), ())), preferred_element_type=jnp.float32,
        )
        wide_ref[2 * step] = product[:, :count]
        wide_ref[2 * step + 1] = product[:, count:]

    for g in range(groups):
        real = wide_ref[:, g, :]
        imag = wide_ref[:, groups + g, :]
        out_ref[g] = jnp.concatenate([real, imag], axis=0).astype(jnp.bfloat16)


def spectra(table, filt, width, groups):
    rows, depth = filt.shape
    count = rows // width
    return pl.pallas_call(
        functools.partial(spectra_kernel, width),
        out_shape=jax.ShapeDtypeStruct((groups, 2 * width, count), jnp.bfloat16),
        in_specs=[pl.BlockSpec(memory_space=pltpu.VMEM)] * 2,
        out_specs=pl.BlockSpec(memory_space=pltpu.VMEM),
        scratch_shapes=[pltpu.VMEM((width, 2 * groups, count), jnp.float32)],
        compiler_params=pltpu.CompilerParams(vmem_limit_bytes=48 * MIB),
        cost_estimate=pl.CostEstimate(
            flops=4 * groups * rows * depth, bytes_accessed=2 * rows * depth, transcendentals=0
        ),
        name="spectra",
    )(table, filt)


def correlate_kernel(width, scale, first, *refs):
    if first:
        tm_ref, own_ref, other_ref, out_ref, real_ref, imag_ref = refs
    else:
        tm_ref, own_ref, other_ref, _, out_ref, real_ref, imag_ref = refs
    groups, _, count = own_ref.shape
    inputs = groups * width
    rows = out_ref.shape[2]
    for at, ref in enumerate((own_ref, other_ref)):
        wide = ref[...].astype(jnp.float32).reshape(groups, 2, width, count)
        real = wide[:, 0].reshape(inputs, count).astype(jnp.bfloat16)
        imag = wide[:, 1].reshape(inputs, count).astype(jnp.bfloat16)
        lanes = slice(at * count, (at + 1) * count)
        real_ref[:, lanes] = real
        imag_ref[:, lanes] = imag
    start = pl.multiple_of(tm_ref[0] * rows, rows)
    contract = (((1,), (1,)), ((), ()))
    dot = functools.partial(lax.dot_general, dimension_numbers=contract, preferred_element_type=jnp.float32)
    step = min(256, rows)
    for at in range(0, rows, step):
        a = real_ref[pl.ds(pl.multiple_of(start + at, step), step), :]
        b = imag_ref[pl.ds(pl.multiple_of(start + at, step), step), :]
        u = real_ref[...]
        w = imag_ref[...]
        out_ref[0, 0, at : at + step] = ((dot(a, u) + dot(b, w)) * scale).astype(jnp.bfloat16)
        out_ref[1, 0, at : at + step] = ((dot(b, u) - dot(a, w)) * scale).astype(jnp.bfloat16)


def correlate(tm, own, other, result, channel, channels, width, parts):
    groups, _, count = own.shape
    inputs = groups * width
    rows = inputs // parts
    scale = 1.0 / (parts * count)
    whole = pl.BlockSpec(own.shape, lambda i: (0, 0, 0))
    args = [tm, own, other]
    in_specs = [pl.BlockSpec(memory_space=pltpu.SMEM), whole, whole]
    aliases = {}
    if result is not None:
        args.append(result)
        in_specs.append(pl.BlockSpec(memory_space=pl.ANY))
        aliases = {3: 0}
    return pl.pallas_call(
        functools.partial(correlate_kernel, width, scale, result is None),
        grid=(1,),
        in_specs=in_specs,
        out_specs=pl.BlockSpec((2, 1, rows, inputs), lambda i: (0, channel, 0, 0)),
        out_shape=jax.ShapeDtypeStruct((2, channels, rows, inputs), jnp.bfloat16),
        scratch_shapes=[pltpu.VMEM((inputs, parts * count), jnp.bfloat16)] * 2,
        input_output_aliases=aliases,
        compiler_params=pltpu.CompilerParams(vmem_limit_bytes=48 * MIB),
        cost_estimate=pl.CostEstimate(
            flops=8 * rows * inputs * parts * count, bytes_accessed=4 * rows * inputs, transcendentals=0
        ),
        name="correlate",
    )(*args)


def after_kernel(*refs):
    pass


def after(block, *earlier):
    return pl.pallas_call(
        after_kernel,
        out_shape=jax.ShapeDtypeStruct(block.shape, block.dtype),
        in_specs=[pl.BlockSpec(memory_space=pl.ANY)] * (1 + len(earlier)),
        out_specs=pl.BlockSpec(memory_space=pl.ANY),
        input_output_aliases={0: 0},
        cost_estimate=pl.CostEstimate(flops=0, bytes_accessed=0, transcendentals=0),
        name="after",
    )(block, *earlier)


def body(voltages, taps):
    width, count, npoints = voltages.shape
    parts = lax.axis_size("tm")
    groups = lax.axis_size("input") * lax.axis_size("freq")
    per_group = CH // groups
    history = passed_along(voltages[:, count - 4 :, :], "tm", 1)
    table = tables(npoints, groups, per_group)
    sums, alts, diffs = filter_bank(voltages, history, taps)
    sources = [sums, diffs, alts, diffs]
    tm = lax.axis_index("tm").astype(jnp.int32).reshape(1)
    own, other = [], []
    for j in range(per_group):
        block = spectra(table[j], sources[j], width, groups)
        if j >= 2:
            block = after(block, other[j - 2])
        block = lax.all_to_all(block, ("input", "freq"), split_axis=0, concat_axis=0, tiled=True)
        own.append(block)
        other.append(swapped(block, "tm"))
    result = None
    for j in range(per_group):
        result = correlate(tm, own[j], other[j], result, j, per_group, width, parts)
    return result


def solution(mesh):
    in_specs = (P(("input", "freq"), "tm", None), P())
    out_specs = P(None, ("input", "freq"), "tm", None)
    return jax.shard_map(body, mesh=mesh, in_specs=in_specs, out_specs=out_specs, check_vma=False)
```

```python
import functools
import math

import jax
import jax.numpy as jnp
from jax import lax
from jax.experimental import pallas as pl
from jax.experimental.pallas import tpu as pltpu
from jax.sharding import PartitionSpec as P

CH = 512
LANES = 128
ROWS = 32
MIB = 1024 * 1024


def passed_along(block, axis, distance):
    devices = range(lax.axis_size(axis))
    route = [(i - distance, i) for i in devices if i - distance in devices]
    return lax.ppermute(block, axis, route)


def swapped(block, axis):
    size = lax.axis_size(axis)
    return lax.ppermute(block, axis, [(i, size - 1 - i) for i in range(size)])


def tables(npoints, order, stride, per_group):
    half, quarter = npoints // 2, npoints // 4
    unit = 2.0 * math.pi / npoints
    sample = lax.broadcasted_iota(jnp.int32, (order.shape[0], quarter), 1)
    angle = ((stride * order[:, None] * sample) % npoints).astype(jnp.float32) * unit
    cos_base, sin_base = jnp.cos(angle), jnp.sin(angle)
    cos_base, sin_base = lax.optimization_barrier((cos_base, sin_base))
    out = [jnp.concatenate([cos_base, -sin_base]).astype(jnp.bfloat16)]
    for j in range(1, per_group):
        depth = quarter if j % 2 == 0 else half
        turn = ((j * jnp.arange(depth, dtype=jnp.int32)) % npoints).astype(jnp.float32) * unit
        cos_turn, sin_turn = jnp.cos(turn), jnp.sin(turn)
        cos_wide = jnp.tile(cos_base, (1, depth // quarter))
        sin_wide = jnp.tile(sin_base, (1, depth // quarter))
        real = cos_wide * cos_turn - sin_wide * sin_turn
        imag = -(sin_wide * cos_turn + cos_wide * sin_turn)
        out.append(jnp.concatenate([real, imag]).astype(jnp.bfloat16))
    return out


def filter_kernel(volt_ref, hist_ref, taps_ref, sum_ref, alt_ref, diff_ref, wide_ref):
    ntaps = taps_ref.shape[0]
    width, count, _ = volt_ref.shape
    quarter = sum_ref.shape[1]
    nhist = hist_ref.shape[1]
    pad = 8
    rows = min(ROWS, count)

    @pl.loop(0, width)
    def _(i):
        for start in range(0, quarter, LANES):
            places = [slice(start + slot * quarter, start + slot * quarter + LANES) for slot in range(4)]
            for slot, lanes in enumerate(places):
                wide_ref[slot, pad - nhist : pad] = hist_ref[i, :, lanes].astype(jnp.float32)
                wide_ref[slot, pad:] = volt_ref[i, :, lanes].astype(jnp.float32)
            for top in range(0, count, rows):
                here = pl.ds(pl.multiple_of(i * count + top, rows), rows)

                def filtered(slot):
                    total = taps_ref[0, places[slot]] * wide_ref[slot, pad + top : pad + top + rows]
                    for lag in range(1, ntaps):
                        first = pad + top - lag
                        total = total + taps_ref[lag, places[slot]] * wide_ref[slot, first : first + rows]
                    return total

                first, third = filtered(0), filtered(2)
                diff_ref[here, places[0]] = (first - third).astype(jnp.bfloat16)
                even = first + third
                second, fourth = filtered(1), filtered(3)
                diff_ref[here, places[1]] = (second - fourth).astype(jnp.bfloat16)
                odd = second + fourth
                sum_ref[here, places[0]] = (even + odd).astype(jnp.bfloat16)
                alt_ref[here, places[0]] = (even - odd).astype(jnp.bfloat16)


def filter_bank(voltages, history, taps):
    width, count, npoints = voltages.shape
    half, quarter = npoints // 2, npoints // 4
    rows = width * count
    depths = (quarter, quarter, half)
    return pl.pallas_call(
        filter_kernel,
        in_specs=[pl.BlockSpec(memory_space=pltpu.VMEM)] * 3,
        out_specs=[pl.BlockSpec(memory_space=pltpu.VMEM)] * 3,
        out_shape=[jax.ShapeDtypeStruct((rows, d), jnp.bfloat16) for d in depths],
        scratch_shapes=[pltpu.VMEM((4, 8 + count, LANES), jnp.float32)],
        compiler_params=pltpu.CompilerParams(vmem_limit_bytes=24 * MIB),
        cost_estimate=pl.CostEstimate(flops=20 * rows * npoints, bytes_accessed=4 * rows * npoints, transcendentals=0),
        name="filter_bank",
    )(voltages, history, taps)


def spectra_kernel(width, table_ref, filt_ref, keep_ref, send_ref, wide_ref):
    rows = filt_ref.shape[0]
    count = rows // width
    groups = keep_ref.shape[0]
    pair = 2 * count
    for step in range(rows // pair):
        product = lax.dot_general(
            table_ref[...], filt_ref[step * pair : (step + 1) * pair, :],
            (((1,), (1,)), ((), ())), preferred_element_type=jnp.float32,
        )
        wide_ref[2 * step] = product[:, :count]
        wide_ref[2 * step + 1] = product[:, count:]

    for at, ref in enumerate((keep_ref, send_ref)):
        for g in range(groups):
            real = wide_ref[:, at * groups + g, :]
            imag = wide_ref[:, (2 + at) * groups + g, :]
            ref[g] = jnp.concatenate([real, imag], axis=0).astype(jnp.bfloat16)


def spectra(table, filt, width, groups):
    rows, depth = filt.shape
    count = rows // width
    return pl.pallas_call(
        functools.partial(spectra_kernel, width),
        out_shape=[jax.ShapeDtypeStruct((groups, 2 * width, count), jnp.bfloat16)] * 2,
        in_specs=[pl.BlockSpec(memory_space=pltpu.VMEM)] * 2,
        out_specs=[pl.BlockSpec(memory_space=pltpu.VMEM)] * 2,
        scratch_shapes=[pltpu.VMEM((width, 4 * groups, count), jnp.float32)],
        compiler_params=pltpu.CompilerParams(vmem_limit_bytes=24 * MIB),
        cost_estimate=pl.CostEstimate(
            flops=8 * groups * rows * depth, bytes_accessed=2 * rows * depth, transcendentals=0
        ),
        name="spectra",
    )(table, filt)


def merge_kernel(units, place_ref, *refs):
    arrays = 2 * len({at for at, _ in units})
    outs = refs[arrays:]
    groups, _, rows, count = outs[0].shape
    width = rows // 2
    low = place_ref[2] == 0
    for side, out_ref in enumerate(outs):
        first_group = 0 if len(outs) == 1 else jnp.bitwise_xor(place_ref[1], side) * groups
        for to, (at, part) in enumerate(units):
            these = (pl.ds(first_group, groups), slice(part * width, (part + 1) * width))
            own = refs[at][these].astype(jnp.float32)
            other = refs[arrays // 2 + at][these].astype(jnp.float32)
            first, second = jnp.where(low, own, other), jnp.where(low, other, own)
            out_ref[:, to] = jnp.concatenate([first, second], axis=1).astype(jnp.bfloat16)


def merge(place, units, own, other, sides):
    channels = sorted({j for j, _ in units})
    places = tuple((channels.index(j), part) for j, part in units)
    arrays = [own[j] for j in channels] + [other[j] for j in channels]
    groups, rows, count = arrays[0].shape
    return pl.pallas_call(
        functools.partial(merge_kernel, places),
        out_shape=[jax.ShapeDtypeStruct((groups // sides, len(units), rows, count), jnp.bfloat16)] * sides,
        in_specs=[pl.BlockSpec(memory_space=pltpu.SMEM)] + [pl.BlockSpec(memory_space=pltpu.VMEM)] * len(arrays),
        out_specs=[pl.BlockSpec(memory_space=pltpu.VMEM)] * sides,
        compiler_params=pltpu.CompilerParams(vmem_limit_bytes=24 * MIB),
        cost_estimate=pl.CostEstimate(
            flops=0, bytes_accessed=4 * len(units) * groups * rows * count, transcendentals=0
        ),
        name="merge",
    )(place, *arrays)


def correlate_kernel(scale, place_ref, *refs):
    out_ref, all_ref, turned_ref = refs[-3:]
    count = refs[0].shape[-1]
    inputs = all_ref.shape[0]
    step = out_ref.shape[2]
    rows = turned_ref.shape[0]
    start = pl.multiple_of(place_ref[0] * rows, rows)

    @pl.when(pl.program_id(0) == 0)
    def _():
        for at in range(4):
            ref = refs[at]
            sides = 1 if len(ref.shape) == 4 else ref.shape[1]
            extent = inputs // sides
            for side in range(sides):
                slot = at ^ side
                lanes = slice(slot * count, (slot + 1) * count)
                if sides == 1:
                    all_ref[:, lanes] = ref[:, 0].reshape(extent, count)
                else:
                    first = jnp.bitwise_xor(place_ref[1], side) * extent
                    here = pl.ds(pl.multiple_of(first, extent), extent)
                    all_ref[here, lanes] = ref[:, side, 0].reshape(extent, count)
        half = 2 * count
        turned_ref[:, :half] = all_ref[pl.ds(start, rows), half:]
        turned_ref[:, half:] = -all_ref[pl.ds(start, rows), :half]

    here = pl.multiple_of(pl.program_id(0) * step, step)
    dot = functools.partial(
        lax.dot_general, dimension_numbers=(((1,), (1,)), ((), ())), preferred_element_type=jnp.float32
    )
    left = all_ref[pl.ds(start + here, step), :]
    out_ref[0, 0] = (dot(left, all_ref[...]) * scale).astype(jnp.bfloat16)
    left = turned_ref[pl.ds(here, step), :]
    out_ref[1, 0] = (dot(left, all_ref[...]) * scale).astype(jnp.bfloat16)


def correlate(place, pieces, result, channel, channels, inputs, parts):
    count = pieces[0][0].shape[-1]
    rows = inputs // parts
    step = min(256, rows)
    scale = 1.0 / (parts * count)
    args = [place]
    in_specs = [pl.BlockSpec(memory_space=pltpu.SMEM)]
    for array, unit in pieces:
        args.append(array)
        lead = array.shape[:-3]
        index = (0,) * len(lead) + (unit, 0, 0)
        in_specs.append(pl.BlockSpec(lead + (1,) + array.shape[-2:], lambda i, index=index: index))
    aliases = {}
    if result is not None:
        aliases = {len(args): 0}
        args.append(result)
        in_specs.append(pl.BlockSpec(memory_space=pl.ANY))
    return pl.pallas_call(
        functools.partial(correlate_kernel, scale),
        grid=(rows // step,),
        in_specs=in_specs,
        out_specs=pl.BlockSpec((2, 1, step, inputs), lambda i: (0, channel, i, 0)),
        out_shape=jax.ShapeDtypeStruct((2, channels, rows, inputs), jnp.bfloat16),
        scratch_shapes=[
            pltpu.VMEM((inputs, 2 * parts * count), jnp.bfloat16),
            pltpu.VMEM((rows, 2 * parts * count), jnp.bfloat16),
        ],
        input_output_aliases=aliases,
        compiler_params=pltpu.CompilerParams(vmem_limit_bytes=24 * MIB),
        cost_estimate=pl.CostEstimate(
            flops=8 * rows * inputs * parts * count, bytes_accessed=4 * rows * inputs, transcendentals=0
        ),
        name="correlate",
    )(*args)


CHUNKS = (((0, 0), (0, 1), (2, 0), (2, 1), (1, 0)), ((1, 1), (3, 0), (3, 1)))
SPLIT = 1


def body(voltages, taps):
    width, count, npoints = voltages.shape
    parts = lax.axis_size("tm")
    groups = lax.axis_size("yh") * lax.axis_size("x") * lax.axis_size("chip")
    cores = lax.axis_size("core")
    per_group = CH // (groups * cores)
    history = passed_along(voltages[:, count - 4 :, :], "tm", 1)
    core = lax.axis_index("core").astype(jnp.int32)
    place = jnp.stack([lax.axis_index("tm").astype(jnp.int32), lax.axis_index("yh").astype(jnp.int32), core])
    half = cores * jnp.arange(groups, dtype=jnp.int32)
    table = tables(npoints, jnp.concatenate([half + core, half + (1 - core)]), per_group, per_group)
    sums, alts, diffs = filter_bank(voltages, history, taps)
    sources = [sums, diffs, alts, diffs]
    own, other, arrived = {}, {}, {}
    for n, units in enumerate(CHUNKS):
        for j in sorted({j for j, _ in units} - set(own)):
            own[j], send = spectra(table[j], sources[j], width, groups)
            other[j] = swapped(send, "core")
        if n == 0:
            (block,) = merge(place, units, own, other, 1)
            axes = ("yh", "x", "chip")
        else:
            here, across = merge(place, units, own, other, 2)
            across = swapped(across, ("yh", "tm"))
            block = jnp.stack([here, across], axis=1)
            axes = ("x", "chip")
        block = lax.all_to_all(block, axes, split_axis=0, concat_axis=0, tiled=True)
        split = SPLIT if n else len(units)
        for first, last in ((0, split), (split, len(units))):
            if first == last:
                continue
            far = block if n == 0 else block[:, :, first:last]
            far = swapped(far, "tm")
            for at in range(first, last):
                arrived[units[at]] = [(block, at), (far, at - first)]
    result = None
    inputs = groups * cores * width
    for j in (0, 2, 1, 3):
        result = correlate(place, arrived[j, 0] + arrived[j, 1], result, j, per_group, inputs, parts)
    return result


def solution(mesh):
    sizes = dict(mesh.shape)
    shape = (2, sizes["input"] // 2, sizes["freq"] // 2, 2, sizes["tm"])
    fine = jax.sharding.Mesh(mesh.devices.reshape(shape), ("yh", "x", "chip", "core", "tm"))
    in_specs = (P(("yh", "x", "chip", "core"), "tm", None), P())
    out_specs = P(None, ("yh", "x", "chip", "core"), "tm", None)
    return jax.shard_map(body, mesh=fine, in_specs=in_specs, out_specs=out_specs, check_vma=False)
```

```python
import functools
import math

import jax
import jax.numpy as jnp
from jax import lax
from jax.experimental import pallas as pl
from jax.experimental.pallas import tpu as pltpu
from jax.sharding import PartitionSpec as P

CH = 512
LANES = 128
ROWS = 32
COLUMNS = 512
MIB = 1024 * 1024


def passed_along(block, axis, distance):
    devices = range(lax.axis_size(axis))
    route = [(i - distance, i) for i in devices if i - distance in devices]
    return lax.ppermute(block, axis, route)


def swapped(block, axis):
    size = lax.axis_size(axis)
    return lax.ppermute(block, axis, [(i, size - 1 - i) for i in range(size)])


def tables(npoints, order, stride, per_group):
    half, quarter = npoints // 2, npoints // 4
    unit = 2.0 * math.pi / npoints
    sample = lax.broadcasted_iota(jnp.int32, (order.shape[0], quarter), 1)
    angle = ((stride * order[:, None] * sample) % npoints).astype(jnp.float32) * unit
    cos_base, sin_base = jnp.cos(angle), jnp.sin(angle)
    cos_base, sin_base = lax.optimization_barrier((cos_base, sin_base))
    out = [jnp.concatenate([cos_base, -sin_base]).astype(jnp.bfloat16)]
    for j in range(1, per_group):
        depth = quarter if j % 2 == 0 else half
        turn = ((j * jnp.arange(depth, dtype=jnp.int32)) % npoints).astype(jnp.float32) * unit
        cos_turn, sin_turn = jnp.cos(turn), jnp.sin(turn)
        cos_wide = jnp.tile(cos_base, (1, depth // quarter))
        sin_wide = jnp.tile(sin_base, (1, depth // quarter))
        real = cos_wide * cos_turn - sin_wide * sin_turn
        imag = -(sin_wide * cos_turn + cos_wide * sin_turn)
        out.append(jnp.concatenate([real, imag]).astype(jnp.bfloat16))
    return out


def filter_kernel(volt_ref, hist_ref, taps_ref, sum_ref, alt_ref, diff_ref, wide_ref):
    ntaps = taps_ref.shape[0]
    width, count, _ = volt_ref.shape
    quarter = sum_ref.shape[1]
    nhist = hist_ref.shape[1]
    pad = 8
    rows = min(ROWS, count)

    @pl.loop(0, width)
    def _(i):
        for start in range(0, quarter, LANES):
            places = [slice(start + slot * quarter, start + slot * quarter + LANES) for slot in range(4)]
            for slot, lanes in enumerate(places):
                wide_ref[slot, pad - nhist : pad] = hist_ref[i, :, lanes].astype(jnp.float32)
                wide_ref[slot, pad:] = volt_ref[i, :, lanes].astype(jnp.float32)
            for top in range(0, count, rows):
                here = pl.ds(pl.multiple_of(i * count + top, rows), rows)

                def filtered(slot):
                    total = taps_ref[0, places[slot]] * wide_ref[slot, pad + top : pad + top + rows]
                    for lag in range(1, ntaps):
                        first = pad + top - lag
                        total = total + taps_ref[lag, places[slot]] * wide_ref[slot, first : first + rows]
                    return total

                first, third = filtered(0), filtered(2)
                diff_ref[here, places[0]] = (first - third).astype(jnp.bfloat16)
                even = first + third
                second, fourth = filtered(1), filtered(3)
                diff_ref[here, places[1]] = (second - fourth).astype(jnp.bfloat16)
                odd = second + fourth
                sum_ref[here, places[0]] = (even + odd).astype(jnp.bfloat16)
                alt_ref[here, places[0]] = (even - odd).astype(jnp.bfloat16)


def filter_bank(voltages, history, taps):
    width, count, npoints = voltages.shape
    half, quarter = npoints // 2, npoints // 4
    rows = width * count
    depths = (quarter, quarter, half)
    return pl.pallas_call(
        filter_kernel,
        in_specs=[pl.BlockSpec(memory_space=pltpu.VMEM)] * 3,
        out_specs=[pl.BlockSpec(memory_space=pltpu.VMEM)] * 3,
        out_shape=[jax.ShapeDtypeStruct((rows, d), jnp.bfloat16) for d in depths],
        scratch_shapes=[pltpu.VMEM((4, 8 + count, LANES), jnp.float32)],
        compiler_params=pltpu.CompilerParams(vmem_limit_bytes=24 * MIB),
        cost_estimate=pl.CostEstimate(flops=20 * rows * npoints, bytes_accessed=4 * rows * npoints, transcendentals=0),
        name="filter_bank",
    )(voltages, history, taps)


def spectra_kernel(width, table_ref, filt_ref, keep_ref, send_ref, wide_ref):
    rows = filt_ref.shape[0]
    count = rows // width
    groups = keep_ref.shape[0]
    pair = 2 * count
    for step in range(rows // pair):
        product = lax.dot_general(
            table_ref[...], filt_ref[step * pair : (step + 1) * pair, :],
            (((1,), (1,)), ((), ())), preferred_element_type=jnp.float32,
        )
        wide_ref[2 * step] = product[:, :count]
        wide_ref[2 * step + 1] = product[:, count:]

    for at, ref in enumerate((keep_ref, send_ref)):
        for g in range(groups):
            real = wide_ref[:, at * groups + g, :]
            imag = wide_ref[:, (2 + at) * groups + g, :]
            ref[g] = jnp.concatenate([real, imag], axis=0).astype(jnp.bfloat16)


def spectra(table, filt, width, groups):
    rows, depth = filt.shape
    count = rows // width
    return pl.pallas_call(
        functools.partial(spectra_kernel, width),
        out_shape=[jax.ShapeDtypeStruct((groups, 2 * width, count), jnp.bfloat16)] * 2,
        in_specs=[pl.BlockSpec(memory_space=pltpu.VMEM)] * 2,
        out_specs=[pl.BlockSpec(memory_space=pltpu.VMEM)] * 2,
        scratch_shapes=[pltpu.VMEM((width, 4 * groups, count), jnp.float32)],
        compiler_params=pltpu.CompilerParams(vmem_limit_bytes=24 * MIB),
        cost_estimate=pl.CostEstimate(
            flops=8 * groups * rows * depth, bytes_accessed=2 * rows * depth, transcendentals=0
        ),
        name="spectra",
    )(table, filt)


def merge_kernel(units, place_ref, *refs):
    arrays = 2 * len({at for at, _ in units})
    out_ref = refs[arrays]
    width = out_ref.shape[2] // 2
    low = place_ref[2] == 0
    for to, (at, part) in enumerate(units):
        these = slice(part * width, (part + 1) * width)
        own = refs[at][:, these].astype(jnp.float32)
        other = refs[arrays // 2 + at][:, these].astype(jnp.float32)
        first, second = jnp.where(low, own, other), jnp.where(low, other, own)
        out_ref[:, to] = jnp.concatenate([first, second], axis=1).astype(jnp.bfloat16)


def split_kernel(units, place_ref, *refs):
    arrays = 2 * len({at for at, _ in units})
    outs = refs[arrays:]
    groups, _, rows, count = outs[0].shape
    width = rows // 2
    low = place_ref[2] == 0
    for side, out_ref in enumerate(outs):
        first_group = jnp.bitwise_xor(place_ref[1], side) * groups
        for to, (at, part) in enumerate(units):
            these = (pl.ds(first_group, groups), slice(part * width, (part + 1) * width))
            own = refs[at][these].astype(jnp.float32)
            other = refs[arrays // 2 + at][these].astype(jnp.float32)
            first, second = jnp.where(low, own, other), jnp.where(low, other, own)
            out_ref[:, to] = jnp.concatenate([first, second], axis=1).astype(jnp.bfloat16)


def merge(place, units, own, other, sides):
    channels = sorted({j for j, _ in units})
    places = tuple((channels.index(j), part) for j, part in units)
    arrays = [own[j] for j in channels] + [other[j] for j in channels]
    groups, rows, count = arrays[0].shape
    cost = pl.CostEstimate(flops=0, bytes_accessed=4 * len(units) * groups * rows * count, transcendentals=0)
    params = pltpu.CompilerParams(vmem_limit_bytes=24 * MIB)
    if sides == 1:
        return pl.pallas_call(
            functools.partial(merge_kernel, places),
            out_shape=[jax.ShapeDtypeStruct((groups, len(units), rows, count), jnp.bfloat16)],
            in_specs=[pl.BlockSpec(memory_space=pltpu.SMEM)] + [pl.BlockSpec(memory_space=pltpu.VMEM)] * len(arrays),
            out_specs=[pl.BlockSpec(memory_space=pltpu.VMEM)],
            compiler_params=params,
            cost_estimate=cost,
            name="merge",
        )(place, *arrays)
    return pl.pallas_call(
        functools.partial(split_kernel, places),
        out_shape=[jax.ShapeDtypeStruct((groups // sides, len(units), rows, count), jnp.bfloat16)] * sides,
        in_specs=[pl.BlockSpec(memory_space=pltpu.SMEM)] + [pl.BlockSpec(memory_space=pltpu.VMEM)] * len(arrays),
        out_specs=[pl.BlockSpec(memory_space=pltpu.VMEM)] * sides,
        compiler_params=params,
        cost_estimate=cost,
        name="split",
    )(place, *arrays)


def correlate_kernel(scale, forms, place_ref, *refs):
    out_ref, all_ref, rows_ref = refs[-3:]
    inputs = all_ref.shape[0]
    rows = rows_ref.shape[0] // 2
    step = out_ref.shape[3]
    half = all_ref.shape[1] // 2
    count = half // 2
    start = pl.multiple_of(place_ref[0] * rows, rows)
    column = pl.program_id(1)
    left = list(refs)

    def gather(parts):
        for part, (form, sources) in enumerate(parts):
            slots = [slice((2 * part + slot) * count, (2 * part + slot + 1) * count) for slot in range(2)]
            if form == "whole":
                for slot in range(2):
                    all_ref[:, slots[slot]] = sources[slot][:, 0].reshape(inputs, count)
                continue
            extent = inputs // 2
            for side in range(2):
                first = jnp.bitwise_xor(place_ref[1], side) * extent
                here = pl.ds(pl.multiple_of(first, extent), extent)
                for slot in range(2):
                    block = sources[0][:, 2 * side + (slot ^ side), 0]
                    all_ref[here, slots[slot]] = block.reshape(extent, count)
        rows_ref[:rows] = all_ref[pl.ds(start, rows), :]
        rows_ref[rows:, :half] = all_ref[pl.ds(start, rows), half:]
        rows_ref[rows:, half:] = -all_ref[pl.ds(start, rows), :half]

    for at, parts in enumerate(forms):
        loaded = [(form, [left.pop(0) for _ in range(many)]) for form, many in parts]

        @pl.when((pl.program_id(0) == at) & (column == 0))
        def _(loaded=loaded):
            gather(loaded)

    here = pl.multiple_of(column * step, step)
    both = lax.dot_general(
        rows_ref[...], all_ref[pl.ds(here, step), :], (((1,), (1,)), ((), ())), preferred_element_type=jnp.float32
    )
    both = (both * scale).astype(jnp.bfloat16)
    out_ref[0, 0] = both[:rows]
    out_ref[1, 0] = both[rows:]


def correlate(place, pieces, result, first, channels, inputs, parts):
    count = pieces[0][0][1][0][0].shape[-1]
    rows = inputs // parts
    step = min(COLUMNS, inputs)
    scale = 1.0 / (parts * count)
    args = [place]
    in_specs = [pl.BlockSpec(memory_space=pltpu.SMEM)]
    for channel in pieces:
        for array, unit in (source for _, sources in channel for source in sources):
            args.append(array)
            lead = array.shape[:-3]
            index = (0,) * len(lead) + (unit, 0, 0)
            in_specs.append(pl.BlockSpec(lead + (1,) + array.shape[-2:], lambda c, i, index=index: index))
    aliases = {}
    if result is not None:
        aliases = {len(args): 0}
        args.append(result)
        in_specs.append(pl.BlockSpec(memory_space=pl.ANY))
    forms = tuple(tuple((form, len(sources)) for form, sources in channel) for channel in pieces)
    return pl.pallas_call(
        functools.partial(correlate_kernel, scale, forms),
        grid=(len(pieces), inputs // step),
        in_specs=in_specs,
        out_specs=pl.BlockSpec((2, 1, rows, step), lambda c, i: (0, first + 2 * c, 0, i)),
        out_shape=jax.ShapeDtypeStruct((2, channels, rows, inputs), jnp.bfloat16),
        scratch_shapes=[
            pltpu.VMEM((inputs, 2 * parts * count), jnp.bfloat16),
            pltpu.VMEM((2 * rows, 2 * parts * count), jnp.bfloat16),
        ],
        input_output_aliases=aliases,
        compiler_params=pltpu.CompilerParams(vmem_limit_bytes=24 * MIB),
        cost_estimate=pl.CostEstimate(
            flops=8 * len(pieces) * rows * inputs * parts * count,
            bytes_accessed=4 * len(pieces) * rows * inputs, transcendentals=0,
        ),
        name="correlate",
    )(*args)


CHUNKS = (((0, 0), (0, 1), (2, 0), (2, 1), (1, 0), (1, 1)), ((3, 0), (3, 1)))
SPLIT = 4
def body(voltages, taps):
    width, count, npoints = voltages.shape
    parts = lax.axis_size("tm")
    groups = lax.axis_size("yh") * lax.axis_size("x") * lax.axis_size("chip")
    cores = lax.axis_size("core")
    per_group = CH // (groups * cores)
    history = passed_along(voltages[:, count - 4 :, :], "tm", 1)
    core = lax.axis_index("core").astype(jnp.int32)
    place = jnp.stack([lax.axis_index("tm").astype(jnp.int32), lax.axis_index("yh").astype(jnp.int32), core])
    half = cores * jnp.arange(groups, dtype=jnp.int32)
    table = tables(npoints, jnp.concatenate([half + core, half + (1 - core)]), per_group, per_group)
    sums, alts, diffs = filter_bank(voltages, history, taps)
    sources = [sums, diffs, alts, diffs]
    own, other, arrived = {}, {}, {}
    for n, units in enumerate(CHUNKS):
        for j in sorted({j for j, _ in units} - set(own)):
            own[j], send = spectra(table[j], sources[j], width, groups)
            other[j] = swapped(send, "core")
        if n == 0:
            (block,) = merge(place, units, own, other, 1)
            block = lax.all_to_all(block, ("yh", "x", "chip"), split_axis=0, concat_axis=0, tiled=True)
            for first, last in ((0, SPLIT), (SPLIT, len(units))):
                far = swapped(block[:, first:last], "tm")
                for at in range(first, last):
                    arrived[units[at]] = ("whole", [(block, at), (far, at - first)])
        else:
            here, across = merge(place, units, own, other, 2)
            across = swapped(across, ("yh", "tm"))
            block = jnp.stack([here, swapped(here, "tm"), across, swapped(across, "tm")], axis=1)
            block = lax.all_to_all(block, ("x", "chip"), split_axis=0, concat_axis=0, tiled=True)
            for at, unit in enumerate(units):
                arrived[unit] = ("sides", [(block, at)])
    result = None
    inputs = groups * cores * width
    for together in ((0, 2), (3,), (1,)):
        pieces = [(arrived[j, 0], arrived[j, 1]) for j in together]
        result = correlate(place, pieces, result, together[0], per_group, inputs, parts)
    return result


def solution(mesh):
    sizes = dict(mesh.shape)
    shape = (2, sizes["input"] // 2, sizes["freq"] // 2, 2, sizes["tm"])
    fine = jax.sharding.Mesh(mesh.devices.reshape(shape), ("yh", "x", "chip", "core", "tm"))
    in_specs = (P(("yh", "x", "chip", "core"), "tm", None), P())
    out_specs = P(None, ("yh", "x", "chip", "core"), "tm", None)
    return jax.shard_map(body, mesh=fine, in_specs=in_specs, out_specs=out_specs, check_vma=False)
```

```python
import functools
import math

import jax
import jax.numpy as jnp
from jax import lax
from jax.experimental import pallas as pl
from jax.experimental.pallas import tpu as pltpu
from jax.sharding import PartitionSpec as P

CH = 512
LANES = 128
ROWS = 32
COLUMNS = 512
WEIGHT = 4
MIB = 1024 * 1024


def passed_along(block, axis, distance):
    devices = range(lax.axis_size(axis))
    route = [(i - distance, i) for i in devices if i - distance in devices]
    return lax.ppermute(block, axis, route)


def swapped(block, axis):
    size = lax.axis_size(axis)
    return lax.ppermute(block, axis, [(i, size - 1 - i) for i in range(size)])


def tables(npoints, order, stride, per_group):
    half, quarter = npoints // 2, npoints // 4
    unit = 2.0 * math.pi / npoints
    sample = lax.broadcasted_iota(jnp.int32, (order.shape[0], quarter), 1)
    angle = ((stride * order[:, None] * sample) % npoints).astype(jnp.float32) * unit
    cos_base, sin_base = jnp.cos(angle), jnp.sin(angle)
    cos_base, sin_base = lax.optimization_barrier((cos_base, sin_base))
    out = [jnp.concatenate([cos_base, -sin_base]).astype(jnp.bfloat16)]
    for j in range(1, per_group):
        depth = quarter if j % 2 == 0 else half
        turn = ((j * jnp.arange(depth, dtype=jnp.int32)) % npoints).astype(jnp.float32) * unit
        cos_turn, sin_turn = jnp.cos(turn), jnp.sin(turn)
        cos_wide = jnp.tile(cos_base, (1, depth // quarter))
        sin_wide = jnp.tile(sin_base, (1, depth // quarter))
        real = cos_wide * cos_turn - sin_wide * sin_turn
        imag = -(sin_wide * cos_turn + cos_wide * sin_turn)
        out.append(jnp.concatenate([real, imag]).astype(jnp.bfloat16))
    return out


def filter_kernel(source_ref, hist_ref, taps_ref, sum_ref, alt_ref, diff_ref, volt_ref, wide_ref, sems):
    ntaps = taps_ref.shape[0]
    width, count, _ = volt_ref.shape
    loads = [pltpu.make_async_copy(source_ref.at[i], volt_ref.at[i], sems.at[i]) for i in range(width)]
    for load in loads:
        load.start()
    quarter = sum_ref.shape[1]
    nhist = hist_ref.shape[1]
    pad = 8
    rows = min(ROWS, count)

    @pl.loop(0, width)
    def _(i):
        pltpu.make_async_copy(source_ref.at[i], volt_ref.at[i], sems.at[i]).wait()
        for start in range(0, quarter, LANES):
            places = [slice(start + slot * quarter, start + slot * quarter + LANES) for slot in range(4)]
            for slot, lanes in enumerate(places):
                wide_ref[slot, pad - nhist : pad] = hist_ref[i, :, lanes].astype(jnp.float32)
                wide_ref[slot, pad:] = volt_ref[i, :, lanes].astype(jnp.float32)
            for top in range(0, count, rows):
                here = pl.ds(pl.multiple_of(i * count + top, rows), rows)

                def filtered(slot):
                    total = taps_ref[0, places[slot]] * wide_ref[slot, pad + top : pad + top + rows]
                    for lag in range(1, ntaps):
                        first = pad + top - lag
                        total = total + taps_ref[lag, places[slot]] * wide_ref[slot, first : first + rows]
                    return total

                first, third = filtered(0), filtered(2)
                diff_ref[here, places[0]] = (first - third).astype(jnp.bfloat16)
                even = first + third
                second, fourth = filtered(1), filtered(3)
                diff_ref[here, places[1]] = (second - fourth).astype(jnp.bfloat16)
                odd = second + fourth
                sum_ref[here, places[0]] = (even + odd).astype(jnp.bfloat16)
                alt_ref[here, places[0]] = (even - odd).astype(jnp.bfloat16)


def filter_bank(voltages, history, taps):
    width, count, npoints = voltages.shape
    half, quarter = npoints // 2, npoints // 4
    rows = width * count
    depths = (quarter, quarter, half)
    return pl.pallas_call(
        filter_kernel,
        in_specs=[pl.BlockSpec(memory_space=pltpu.HBM)] + [pl.BlockSpec(memory_space=pltpu.VMEM)] * 2,
        out_specs=[pl.BlockSpec(memory_space=pltpu.VMEM)] * 3,
        out_shape=[jax.ShapeDtypeStruct((rows, d), jnp.bfloat16) for d in depths],
        scratch_shapes=[
            pltpu.VMEM(voltages.shape, voltages.dtype),
            pltpu.VMEM((4, 8 + count, LANES), jnp.float32),
            pltpu.SemaphoreType.DMA((width,)),
        ],
        compiler_params=pltpu.CompilerParams(vmem_limit_bytes=24 * MIB),
        cost_estimate=pl.CostEstimate(flops=20 * rows * npoints, bytes_accessed=4 * rows * npoints, transcendentals=0),
        name="filter_bank",
    )(voltages, history, taps)


def spectra_kernel(width, table_ref, filt_ref, keep_ref, send_ref, wide_ref):
    rows = filt_ref.shape[0]
    count = rows // width
    groups = keep_ref.shape[0]
    pair = 2 * count
    for step in range(rows // pair):
        product = lax.dot_general(
            table_ref[...], filt_ref[step * pair : (step + 1) * pair, :],
            (((1,), (1,)), ((), ())), preferred_element_type=jnp.float32,
        )
        wide_ref[2 * step] = product[:, :count]
        wide_ref[2 * step + 1] = product[:, count:]

    for at, ref in enumerate((keep_ref, send_ref)):
        for g in range(groups):
            real = wide_ref[:, at * groups + g, :]
            imag = wide_ref[:, (2 + at) * groups + g, :]
            ref[g] = jnp.concatenate([real, imag], axis=0).astype(jnp.bfloat16)


def spectra(table, filt, width, groups):
    rows, depth = filt.shape
    count = rows // width
    return pl.pallas_call(
        functools.partial(spectra_kernel, width),
        out_shape=[jax.ShapeDtypeStruct((groups, 2 * width, count), jnp.bfloat16)] * 2,
        in_specs=[pl.BlockSpec(memory_space=pltpu.VMEM)] * 2,
        out_specs=[pl.BlockSpec(memory_space=pltpu.VMEM)] * 2,
        scratch_shapes=[pltpu.VMEM((width, 4 * groups, count), jnp.float32)],
        compiler_params=pltpu.CompilerParams(vmem_limit_bytes=24 * MIB),
        cost_estimate=pl.CostEstimate(
            flops=8 * groups * rows * depth, bytes_accessed=2 * rows * depth, transcendentals=0
        ),
        name="spectra",
    )(table, filt)


def merge_kernel(units, place_ref, *refs):
    arrays = 2 * len({at for at, _ in units})
    out_ref = refs[-1]
    width = out_ref.shape[2] // 2
    low = place_ref[2] == 0
    for to, (at, part) in enumerate(units):
        these = slice(part * width, (part + 1) * width)
        own = refs[at][:, these].astype(jnp.float32)
        other = refs[arrays // 2 + at][:, these].astype(jnp.float32)
        first, second = jnp.where(low, own, other), jnp.where(low, other, own)
        out_ref[:, to] = jnp.concatenate([first, second], axis=1).astype(jnp.bfloat16)


def split_kernel(units, place_ref, *refs):
    arrays = 2 * len({at for at, _ in units})
    outs = refs[arrays:]
    groups, _, rows, count = outs[0].shape
    width = rows // 2
    low = place_ref[2] == 0
    for side, out_ref in enumerate(outs):
        first_group = jnp.bitwise_xor(place_ref[1], side) * groups
        for to, (at, part) in enumerate(units):
            these = (pl.ds(first_group, groups), slice(part * width, (part + 1) * width))
            own = refs[at][these].astype(jnp.float32)
            other = refs[arrays // 2 + at][these].astype(jnp.float32)
            first, second = jnp.where(low, own, other), jnp.where(low, other, own)
            out_ref[:, to] = jnp.concatenate([first, second], axis=1).astype(jnp.bfloat16)


def merge_into(place, units, own, other, result, first, total):
    channels = sorted({j for j, _ in units})
    places = tuple((channels.index(j), part) for j, part in units)
    arrays = [own[j] for j in channels] + [other[j] for j in channels]
    groups, rows, count = arrays[0].shape
    whole = pl.BlockSpec((groups, rows, count), lambda i: (0, 0, 0))
    in_specs = [pl.BlockSpec(memory_space=pltpu.SMEM)] + [whole] * len(arrays)
    args, aliases = [place] + arrays, {}
    if result is not None:
        aliases = {len(args): 0}
        args.append(result)
        in_specs.append(pl.BlockSpec(memory_space=pl.ANY))
    return pl.pallas_call(
        functools.partial(merge_kernel, places),
        grid=(1,),
        out_shape=jax.ShapeDtypeStruct((groups, total, rows, count), jnp.bfloat16),
        in_specs=in_specs,
        out_specs=pl.BlockSpec((groups, len(units), rows, count), lambda i: (0, first // len(units), 0, 0)),
        input_output_aliases=aliases,
        compiler_params=pltpu.CompilerParams(vmem_limit_bytes=24 * MIB),
        cost_estimate=pl.CostEstimate(
            flops=0, bytes_accessed=4 * len(units) * groups * rows * count, transcendentals=0
        ),
        name="merge",
    )(*args)


def split(place, units, own, other):
    channels = sorted({j for j, _ in units})
    places = tuple((channels.index(j), part) for j, part in units)
    arrays = [own[j] for j in channels] + [other[j] for j in channels]
    groups, rows, count = arrays[0].shape
    cost = pl.CostEstimate(flops=0, bytes_accessed=4 * len(units) * groups * rows * count, transcendentals=0)
    params = pltpu.CompilerParams(vmem_limit_bytes=24 * MIB)
    return pl.pallas_call(
        functools.partial(split_kernel, places),
        out_shape=[jax.ShapeDtypeStruct((groups // 2, len(units), rows, count), jnp.bfloat16)] * 2,
        in_specs=[pl.BlockSpec(memory_space=pltpu.SMEM)] + [pl.BlockSpec(memory_space=pltpu.VMEM)] * len(arrays),
        out_specs=[pl.BlockSpec(memory_space=pltpu.VMEM)] * 2,
        compiler_params=params,
        cost_estimate=cost,
        name="split",
    )(place, *arrays)


def correlate_kernel(scale, forms, place_ref, *refs):
    out_ref, all_ref, rows_ref = refs[-3:]
    inputs = all_ref.shape[0]
    rows = rows_ref.shape[0] // 2
    step = out_ref.shape[3]
    half = all_ref.shape[1] // 2
    count = half // 2
    start = pl.multiple_of(place_ref[0] * rows, rows)
    column = pl.program_id(1)
    left = list(refs)

    def gather(parts):
        for part, (form, sources) in enumerate(parts):
            slots = [slice((2 * part + slot) * count, (2 * part + slot + 1) * count) for slot in range(2)]
            if form == "whole":
                for slot in range(2):
                    all_ref[:, slots[slot]] = sources[slot][:, 0].reshape(inputs, count)
                continue
            extent = inputs // 2
            for side in range(2):
                first = jnp.bitwise_xor(place_ref[1], side) * extent
                here = pl.ds(pl.multiple_of(first, extent), extent)
                for slot in range(2):
                    block = sources[0][:, 2 * side + (slot ^ side), 0]
                    all_ref[here, slots[slot]] = block.reshape(extent, count)
        rows_ref[:rows] = all_ref[pl.ds(start, rows), :]
        rows_ref[rows:, :half] = all_ref[pl.ds(start, rows), half:]
        rows_ref[rows:, half:] = -all_ref[pl.ds(start, rows), :half]

    for at, parts in enumerate(forms):
        loaded = [(form, [left.pop(0) for _ in range(many)]) for form, many in parts]

        @pl.when((pl.program_id(0) == at) & (column == 0))
        def _(loaded=loaded):
            gather(loaded)

    here = pl.multiple_of(column * step, step)
    both = lax.dot_general(
        rows_ref[...], all_ref[pl.ds(here, step), :], (((1,), (1,)), ((), ())), preferred_element_type=jnp.float32
    )
    both = (both * scale).astype(jnp.bfloat16)
    out_ref[0, 0] = both[:rows]
    out_ref[1, 0] = both[rows:]


def correlate(place, pieces, result, first, channels, inputs, parts):
    count = pieces[0][0][1][0][0].shape[-1]
    rows = inputs // parts
    step = min(COLUMNS, inputs)
    scale = 1.0 / (parts * count)
    args = [place]
    in_specs = [pl.BlockSpec(memory_space=pltpu.SMEM)]
    for channel in pieces:
        for array, unit in (source for _, sources in channel for source in sources):
            args.append(array)
            lead = array.shape[:-3]
            index = (0,) * len(lead) + (unit, 0, 0)
            in_specs.append(pl.BlockSpec(lead + (1,) + array.shape[-2:], lambda c, i, index=index: index))
    aliases = {}
    if result is not None:
        aliases = {len(args): 0}
        args.append(result)
        in_specs.append(pl.BlockSpec(memory_space=pl.ANY))
    forms = tuple(tuple((form, len(sources)) for form, sources in channel) for channel in pieces)
    return pl.pallas_call(
        functools.partial(correlate_kernel, scale, forms),
        grid=(len(pieces), inputs // step),
        in_specs=in_specs,
        out_specs=pl.BlockSpec((2, 1, rows, step), lambda c, i: (0, first + 2 * c, 0, i)),
        out_shape=jax.ShapeDtypeStruct((2, channels, rows, inputs), jnp.bfloat16),
        scratch_shapes=[
            pltpu.VMEM((inputs, 2 * parts * count), jnp.bfloat16),
            pltpu.VMEM((2 * rows, 2 * parts * count), jnp.bfloat16),
        ],
        input_output_aliases=aliases,
        compiler_params=pltpu.CompilerParams(vmem_limit_bytes=24 * MIB),
        cost_estimate=pl.CostEstimate(
            flops=WEIGHT * 8 * len(pieces) * rows * inputs * parts * count,
            bytes_accessed=4 * len(pieces) * rows * inputs, transcendentals=0,
        ),
        name="correlate",
    )(*args)


CHUNKS = (((0, 0), (0, 1), (2, 0), (2, 1), (1, 0), (1, 1)), ((3, 0), (3, 1)))
SPLIT = 4
def body(voltages, taps):
    width, count, npoints = voltages.shape
    parts = lax.axis_size("tm")
    groups = lax.axis_size("yh") * lax.axis_size("x") * lax.axis_size("chip")
    cores = lax.axis_size("core")
    per_group = CH // (groups * cores)
    history = passed_along(voltages[:, count - 4 :, :], "tm", 1)
    core = lax.axis_index("core").astype(jnp.int32)
    place = jnp.stack([lax.axis_index("tm").astype(jnp.int32), lax.axis_index("yh").astype(jnp.int32), core])
    half = cores * jnp.arange(groups, dtype=jnp.int32)
    table = tables(npoints, jnp.concatenate([half + core, half + (1 - core)]), per_group, per_group)
    sums, alts, diffs = filter_bank(voltages, history, taps)
    sources = [sums, diffs, alts, diffs]
    own, other, arrived = {}, {}, {}
    for n, units in enumerate(CHUNKS):
        for j in sorted({j for j, _ in units} - set(own)):
            own[j], send = spectra(table[j], sources[j], width, groups)
            other[j] = swapped(send, "core")
        if n == 0:
            block = merge_into(place, units[:SPLIT], own, other, None, 0, len(units))
            block = merge_into(place, units[SPLIT:], own, other, block, SPLIT, len(units))
            block = lax.all_to_all(block, ("yh", "x", "chip"), split_axis=0, concat_axis=0, tiled=True)
            for first, last in ((0, SPLIT), (SPLIT, len(units))):
                far = swapped(block[:, first:last], "tm")
                for at in range(first, last):
                    arrived[units[at]] = ("whole", [(block, at), (far, at - first)])
        else:
            here, across = split(place, units, own, other)
            across = swapped(across, ("yh", "tm"))
            block = jnp.stack([here, swapped(here, "tm"), across, swapped(across, "tm")], axis=1)
            block = lax.all_to_all(block, ("x", "chip"), split_axis=0, concat_axis=0, tiled=True)
            for at, unit in enumerate(units):
                arrived[unit] = ("sides", [(block, at)])
    result = None
    inputs = groups * cores * width
    for together in ((0, 2), (1,), (3,)):
        pieces = [(arrived[j, 0], arrived[j, 1]) for j in together]
        result = correlate(place, pieces, result, together[0], per_group, inputs, parts)
    return result


def solution(mesh):
    sizes = dict(mesh.shape)
    shape = (2, sizes["input"] // 2, sizes["freq"] // 2, 2, sizes["tm"])
    fine = jax.sharding.Mesh(mesh.devices.reshape(shape), ("yh", "x", "chip", "core", "tm"))
    in_specs = (P(("yh", "x", "chip", "core"), "tm", None), P())
    out_specs = P(None, ("yh", "x", "chip", "core"), "tm", None)
    return jax.shard_map(body, mesh=fine, in_specs=in_specs, out_specs=out_specs, check_vma=False)
```

```python
import functools
import math

import jax
import jax.numpy as jnp
from jax import lax
from jax.experimental import pallas as pl
from jax.experimental.pallas import tpu as pltpu
from jax.sharding import PartitionSpec as P

CH = 512
LANES = 128
ROWS = 32
COLUMNS = 1024
WEIGHT = 4
MIB = 1024 * 1024


def passed_along(block, axis, distance):
    devices = range(lax.axis_size(axis))
    route = [(i - distance, i) for i in devices if i - distance in devices]
    return lax.ppermute(block, axis, route)


def swapped(block, axis):
    size = lax.axis_size(axis)
    return lax.ppermute(block, axis, [(i, size - 1 - i) for i in range(size)])


def tables(npoints, order, stride, per_group):
    half, quarter = npoints // 2, npoints // 4
    unit = 2.0 * math.pi / npoints
    sample = lax.broadcasted_iota(jnp.int32, (order.shape[0], quarter), 1)
    angle = ((stride * order[:, None] * sample) % npoints).astype(jnp.float32) * unit
    cos_base, sin_base = jnp.cos(angle), jnp.sin(angle)
    cos_base, sin_base = lax.optimization_barrier((cos_base, sin_base))
    out = [jnp.concatenate([cos_base, -sin_base]).astype(jnp.bfloat16)]
    for j in range(1, per_group):
        depth = quarter if j % 2 == 0 else half
        turn = ((j * jnp.arange(depth, dtype=jnp.int32)) % npoints).astype(jnp.float32) * unit
        cos_turn, sin_turn = jnp.cos(turn), jnp.sin(turn)
        cos_wide = jnp.tile(cos_base, (1, depth // quarter))
        sin_wide = jnp.tile(sin_base, (1, depth // quarter))
        real = cos_wide * cos_turn - sin_wide * sin_turn
        imag = -(sin_wide * cos_turn + cos_wide * sin_turn)
        out.append(jnp.concatenate([real, imag]).astype(jnp.bfloat16))
    return out


def filter_kernel(source_ref, hist_ref, taps_ref, sum_ref, alt_ref, diff_ref, volt_ref, wide_ref, sems):
    ntaps = taps_ref.shape[0]
    width, count, _ = volt_ref.shape
    loads = [pltpu.make_async_copy(source_ref.at[i], volt_ref.at[i], sems.at[i]) for i in range(width)]
    for load in loads:
        load.start()
    quarter = sum_ref.shape[1]
    nhist = hist_ref.shape[1]
    pad = 8
    rows = min(ROWS, count)

    @pl.loop(0, width)
    def _(i):
        pltpu.make_async_copy(source_ref.at[i], volt_ref.at[i], sems.at[i]).wait()
        for start in range(0, quarter, LANES):
            places = [slice(start + slot * quarter, start + slot * quarter + LANES) for slot in range(4)]
            for slot, lanes in enumerate(places):
                wide_ref[slot, pad - nhist : pad] = hist_ref[i, :, lanes].astype(jnp.float32)
                wide_ref[slot, pad:] = volt_ref[i, :, lanes].astype(jnp.float32)
            for top in range(0, count, rows):
                here = pl.ds(pl.multiple_of(i * count + top, rows), rows)

                def filtered(slot):
                    total = taps_ref[0, places[slot]] * wide_ref[slot, pad + top : pad + top + rows]
                    for lag in range(1, ntaps):
                        first = pad + top - lag
                        total = total + taps_ref[lag, places[slot]] * wide_ref[slot, first : first + rows]
                    return total

                first, third = filtered(0), filtered(2)
                diff_ref[here, places[0]] = (first - third).astype(jnp.bfloat16)
                even = first + third
                second, fourth = filtered(1), filtered(3)
                diff_ref[here, places[1]] = (second - fourth).astype(jnp.bfloat16)
                odd = second + fourth
                sum_ref[here, places[0]] = (even + odd).astype(jnp.bfloat16)
                alt_ref[here, places[0]] = (even - odd).astype(jnp.bfloat16)


def filter_bank(voltages, history, taps):
    width, count, npoints = voltages.shape
    half, quarter = npoints // 2, npoints // 4
    rows = width * count
    depths = (quarter, quarter, half)
    return pl.pallas_call(
        filter_kernel,
        in_specs=[pl.BlockSpec(memory_space=pltpu.HBM)] + [pl.BlockSpec(memory_space=pltpu.VMEM)] * 2,
        out_specs=[pl.BlockSpec(memory_space=pltpu.VMEM)] * 3,
        out_shape=[jax.ShapeDtypeStruct((rows, d), jnp.bfloat16) for d in depths],
        scratch_shapes=[
            pltpu.VMEM(voltages.shape, voltages.dtype),
            pltpu.VMEM((4, 8 + count, LANES), jnp.float32),
            pltpu.SemaphoreType.DMA((width,)),
        ],
        compiler_params=pltpu.CompilerParams(vmem_limit_bytes=24 * MIB),
        cost_estimate=pl.CostEstimate(flops=20 * rows * npoints, bytes_accessed=4 * rows * npoints, transcendentals=0),
        name="filter_bank",
    )(voltages, history, taps)


def spectra_kernel(width, table_ref, filt_ref, keep_ref, send_ref, wide_ref):
    rows = filt_ref.shape[0]
    count = rows // width
    groups = keep_ref.shape[0]
    pair = 2 * count
    for step in range(rows // pair):
        product = lax.dot_general(
            table_ref[...], filt_ref[step * pair : (step + 1) * pair, :],
            (((1,), (1,)), ((), ())), preferred_element_type=jnp.float32,
        )
        wide_ref[2 * step] = product[:, :count]
        wide_ref[2 * step + 1] = product[:, count:]

    for at, ref in enumerate((keep_ref, send_ref)):
        for g in range(groups):
            real = wide_ref[:, at * groups + g, :]
            imag = wide_ref[:, (2 + at) * groups + g, :]
            ref[g] = jnp.concatenate([real, imag], axis=0).astype(jnp.bfloat16)


def spectra(table, filt, width, groups):
    rows, depth = filt.shape
    count = rows // width
    return pl.pallas_call(
        functools.partial(spectra_kernel, width),
        out_shape=[jax.ShapeDtypeStruct((groups, 2 * width, count), jnp.bfloat16)] * 2,
        in_specs=[pl.BlockSpec(memory_space=pltpu.VMEM)] * 2,
        out_specs=[pl.BlockSpec(memory_space=pltpu.VMEM)] * 2,
        scratch_shapes=[pltpu.VMEM((width, 4 * groups, count), jnp.float32)],
        compiler_params=pltpu.CompilerParams(vmem_limit_bytes=24 * MIB),
        cost_estimate=pl.CostEstimate(
            flops=8 * groups * rows * depth, bytes_accessed=2 * rows * depth, transcendentals=0
        ),
        name="spectra",
    )(table, filt)


def merge_kernel(units, place_ref, *refs):
    arrays = 2 * len({at for at, _ in units})
    out_ref = refs[-1]
    width = out_ref.shape[2] // 2
    low = place_ref[2] == 0
    for to, (at, part) in enumerate(units):
        these = slice(part * width, (part + 1) * width)
        own = refs[at][:, these].astype(jnp.float32)
        other = refs[arrays // 2 + at][:, these].astype(jnp.float32)
        first, second = jnp.where(low, own, other), jnp.where(low, other, own)
        out_ref[:, to] = jnp.concatenate([first, second], axis=1).astype(jnp.bfloat16)


def split_kernel(units, place_ref, *refs):
    arrays = 2 * len({at for at, _ in units})
    outs = refs[arrays:]
    groups, _, rows, count = outs[0].shape
    width = rows // 2
    low = place_ref[2] == 0
    for side, out_ref in enumerate(outs):
        first_group = jnp.bitwise_xor(place_ref[1], side) * groups
        for to, (at, part) in enumerate(units):
            these = (pl.ds(first_group, groups), slice(part * width, (part + 1) * width))
            own = refs[at][these].astype(jnp.float32)
            other = refs[arrays // 2 + at][these].astype(jnp.float32)
            first, second = jnp.where(low, own, other), jnp.where(low, other, own)
            out_ref[:, to] = jnp.concatenate([first, second], axis=1).astype(jnp.bfloat16)


def merge_into(place, units, own, other, result, first, total):
    channels = sorted({j for j, _ in units})
    places = tuple((channels.index(j), part) for j, part in units)
    arrays = [own[j] for j in channels] + [other[j] for j in channels]
    groups, rows, count = arrays[0].shape
    whole = pl.BlockSpec((groups, rows, count), lambda i: (0, 0, 0))
    in_specs = [pl.BlockSpec(memory_space=pltpu.SMEM)] + [whole] * len(arrays)
    args, aliases = [place] + arrays, {}
    if result is not None:
        aliases = {len(args): 0}
        args.append(result)
        in_specs.append(pl.BlockSpec(memory_space=pl.ANY))
    return pl.pallas_call(
        functools.partial(merge_kernel, places),
        grid=(1,),
        out_shape=jax.ShapeDtypeStruct((groups, total, rows, count), jnp.bfloat16),
        in_specs=in_specs,
        out_specs=pl.BlockSpec((groups, len(units), rows, count), lambda i: (0, first // len(units), 0, 0)),
        input_output_aliases=aliases,
        compiler_params=pltpu.CompilerParams(vmem_limit_bytes=24 * MIB),
        cost_estimate=pl.CostEstimate(
            flops=0, bytes_accessed=4 * len(units) * groups * rows * count, transcendentals=0
        ),
        name="merge",
    )(*args)


def split(place, units, own, other):
    channels = sorted({j for j, _ in units})
    places = tuple((channels.index(j), part) for j, part in units)
    arrays = [own[j] for j in channels] + [other[j] for j in channels]
    groups, rows, count = arrays[0].shape
    cost = pl.CostEstimate(flops=0, bytes_accessed=4 * len(units) * groups * rows * count, transcendentals=0)
    params = pltpu.CompilerParams(vmem_limit_bytes=24 * MIB)
    return pl.pallas_call(
        functools.partial(split_kernel, places),
        out_shape=[jax.ShapeDtypeStruct((groups // 2, len(units), rows, count), jnp.bfloat16)] * 2,
        in_specs=[pl.BlockSpec(memory_space=pltpu.SMEM)] + [pl.BlockSpec(memory_space=pltpu.VMEM)] * len(arrays),
        out_specs=[pl.BlockSpec(memory_space=pltpu.VMEM)] * 2,
        compiler_params=params,
        cost_estimate=cost,
        name="split",
    )(place, *arrays)


def correlate_kernel(scale, forms, place_ref, *refs):
    out_ref, all_ref, rows_ref = refs[-3:]
    inputs = all_ref.shape[0]
    rows = rows_ref.shape[0] // 2
    step = out_ref.shape[3]
    half = all_ref.shape[1] // 2
    count = half // 2
    start = pl.multiple_of(place_ref[0] * rows, rows)
    column = pl.program_id(1)
    left = list(refs)

    def gather(parts):
        for part, (form, sources) in enumerate(parts):
            slots = [slice((2 * part + slot) * count, (2 * part + slot + 1) * count) for slot in range(2)]
            if form == "whole":
                for slot in range(2):
                    all_ref[:, slots[slot]] = sources[slot][:, 0].reshape(inputs, count)
                continue
            extent = inputs // 2
            for side in range(2):
                first = jnp.bitwise_xor(place_ref[1], side) * extent
                here = pl.ds(pl.multiple_of(first, extent), extent)
                for slot in range(2):
                    block = sources[0][:, 2 * side + (slot ^ side), 0]
                    all_ref[here, slots[slot]] = block.reshape(extent, count)
        rows_ref[:rows] = all_ref[pl.ds(start, rows), :]
        rows_ref[rows:, :half] = all_ref[pl.ds(start, rows), half:]
        rows_ref[rows:, half:] = -all_ref[pl.ds(start, rows), :half]

    for at, parts in enumerate(forms):
        loaded = [(form, [left.pop(0) for _ in range(many)]) for form, many in parts]

        @pl.when((pl.program_id(0) == at) & (column == 0))
        def _(loaded=loaded):
            gather(loaded)

    here = pl.multiple_of(column * step, step)
    both = lax.dot_general(
        rows_ref[...], all_ref[pl.ds(here, step), :], (((1,), (1,)), ((), ())), preferred_element_type=jnp.float32
    )
    both = (both * scale).astype(jnp.bfloat16)
    out_ref[0, 0] = both[:rows]
    out_ref[1, 0] = both[rows:]


def correlate(place, pieces, result, first, channels, inputs, parts):
    count = pieces[0][0][1][0][0].shape[-1]
    rows = inputs // parts
    step = min(COLUMNS, inputs)
    scale = 1.0 / (parts * count)
    args = [place]
    in_specs = [pl.BlockSpec(memory_space=pltpu.SMEM)]
    for channel in pieces:
        for array, unit in (source for _, sources in channel for source in sources):
            args.append(array)
            lead = array.shape[:-3]
            index = (0,) * len(lead) + (unit, 0, 0)
            in_specs.append(pl.BlockSpec(lead + (1,) + array.shape[-2:], lambda c, i, index=index: index))
    aliases = {}
    if result is not None:
        aliases = {len(args): 0}
        args.append(result)
        in_specs.append(pl.BlockSpec(memory_space=pl.ANY))
    forms = tuple(tuple((form, len(sources)) for form, sources in channel) for channel in pieces)
    return pl.pallas_call(
        functools.partial(correlate_kernel, scale, forms),
        grid=(len(pieces), inputs // step),
        in_specs=in_specs,
        out_specs=pl.BlockSpec((2, 1, rows, step), lambda c, i: (0, first + 2 * c, 0, i)),
        out_shape=jax.ShapeDtypeStruct((2, channels, rows, inputs), jnp.bfloat16),
        scratch_shapes=[
            pltpu.VMEM((inputs, 2 * parts * count), jnp.bfloat16),
            pltpu.VMEM((2 * rows, 2 * parts * count), jnp.bfloat16),
        ],
        input_output_aliases=aliases,
        compiler_params=pltpu.CompilerParams(vmem_limit_bytes=24 * MIB),
        cost_estimate=pl.CostEstimate(
            flops=WEIGHT * 8 * len(pieces) * rows * inputs * parts * count,
            bytes_accessed=4 * len(pieces) * rows * inputs, transcendentals=0,
        ),
        name="correlate",
    )(*args)


CHUNKS = (((0, 0), (0, 1), (2, 0), (2, 1), (1, 0), (1, 1)), ((3, 0), (3, 1)))
SPLIT = 4
def body(voltages, taps):
    width, count, npoints = voltages.shape
    parts = lax.axis_size("tm")
    groups = lax.axis_size("yh") * lax.axis_size("x") * lax.axis_size("chip")
    cores = lax.axis_size("core")
    per_group = CH // (groups * cores)
    history = passed_along(voltages[:, count - 4 :, :], "tm", 1)
    core = lax.axis_index("core").astype(jnp.int32)
    place = jnp.stack([lax.axis_index("tm").astype(jnp.int32), lax.axis_index("yh").astype(jnp.int32), core])
    half = cores * jnp.arange(groups, dtype=jnp.int32)
    table = tables(npoints, jnp.concatenate([half + core, half + (1 - core)]), per_group, per_group)
    sums, alts, diffs = filter_bank(voltages, history, taps)
    sources = [sums, diffs, alts, diffs]
    own, other, arrived = {}, {}, {}
    for n, units in enumerate(CHUNKS):
        for j in sorted({j for j, _ in units} - set(own)):
            own[j], send = spectra(table[j], sources[j], width, groups)
            other[j] = swapped(send, "core")
        if n == 0:
            block = merge_into(place, units[:SPLIT], own, other, None, 0, len(units))
            block = merge_into(place, units[SPLIT:], own, other, block, SPLIT, len(units))
            block = lax.all_to_all(block, ("yh", "x", "chip"), split_axis=0, concat_axis=0, tiled=True)
            for first, last in ((0, SPLIT), (SPLIT, len(units))):
                far = swapped(block[:, first:last], "tm")
                for at in range(first, last):
                    arrived[units[at]] = ("whole", [(block, at), (far, at - first)])
        else:
            here, across = split(place, units, own, other)
            across = swapped(across, ("yh", "tm"))
            block = jnp.stack([here, swapped(here, "tm"), across, swapped(across, "tm")], axis=1)
            block = lax.all_to_all(block, ("x", "chip"), split_axis=0, concat_axis=0, tiled=True)
            for at, unit in enumerate(units):
                arrived[unit] = ("sides", [(block, at)])
    result = None
    inputs = groups * cores * width
    for together in ((0, 2), (1,), (3,)):
        pieces = [(arrived[j, 0], arrived[j, 1]) for j in together]
        result = correlate(place, pieces, result, together[0], per_group, inputs, parts)
    return result


def solution(mesh):
    sizes = dict(mesh.shape)
    shape = (2, sizes["input"] // 2, sizes["freq"] // 2, 2, sizes["tm"])
    fine = jax.sharding.Mesh(mesh.devices.reshape(shape), ("yh", "x", "chip", "core", "tm"))
    in_specs = (P(("yh", "x", "chip", "core"), "tm", None), P())
    out_specs = P(None, ("yh", "x", "chip", "core"), "tm", None)
    return jax.shard_map(body, mesh=fine, in_specs=in_specs, out_specs=out_specs, check_vma=False)
```
